512 devices in a mesh: sub: 64 (over z, x), beam: 8 (over y, core).
Axes of the slice: x: 4, y: 4, z: 16, core: 2. Of those that a mesh axis runs over, the one named last changes fastest.
Arguments:
- intensity: float32 [16, 8192, 256], P(None, ('sub', 'beam')), may hold values from -6 to 6
- shift_table: int32 [11, 2048], replicated, may hold values from 0 to 154, as said below
- box_widths: int32 [8], replicated, may hold values from 1 to 64, as said below
Outputs:
- dm_plane: float32 [16, 2048, 256], P('beam', 'sub')
- peaks: float32 [16, 16, 2048], P('beam', None, 'sub')
The draws below stay inside these ranges and needn't reach their ends.
Inputs may be any that keep to these rules, and one draw needn't show every extreme that they name: `shift_table`: entry (l, d) is the delay in samples given to the upper half at level l + 1 for DM row d; it rises with d up to a dither of one sample, and entries with d at or over 2^(l + 1) are not read. `box_widths`: 8 different widths; 1 and 64 are always among them.
All inputs are finite; a program needn't handle non-finite values.
Results may differ from the reference program's by a relative error of at most 0.00013.
Values sent between devices are 32-bit elements; how exact they have to be, the bound alone decides.
No kernel may reach another device: no remote copies, remote signals or barrier semaphores. Data moves between devices by JAX's collectives and lax.ppermute only.
A program may use at most 64 MiB of HBM per device.

```python
import jax
import jax.numpy as jnp
from jax import lax

CHAN = 8192
GROUP = 4
SUBS = 2048
LEVELS = 11
BEAMS = 16
TIME = 256
NBOX = 8
GTAPS = 64
N_SUB = 64


def draw_shift_table(key, part):
    rate_key = jax.random.fold_in(key, 11)
    step_key = jax.random.fold_in(key, 23)
    rates = jax.random.randint(rate_key, (LEVELS, 1), 40, 61)
    rates = rates.at[LEVELS - 1, 0].set(60)
    dither = jax.random.randint(step_key, (LEVELS, SUBS), 0, 2)
    dither = dither.at[:, SUBS - 1].set(1)
    rows = jnp.arange(SUBS, dtype=jnp.int32)[None, :]
    return (rows * (TIME * rates) // (SUBS * 100) + dither).astype(jnp.int32)


def draw_box_widths(key, part):
    middle = jax.random.permutation(jax.random.fold_in(key, 5), 62)[:NBOX - 2] + 2
    both = jnp.concatenate([jnp.array([1, 64], dtype=jnp.int32), middle.astype(jnp.int32)])
    return jax.random.permutation(jax.random.fold_in(key, 7), both).astype(jnp.int32)


def block_scale(rng, dims, cuts, smallest, high):
    def one(dim, parts):
        steps = jax.random.uniform(jax.random.fold_in(jax.random.fold_in(rng, 6), dim), (parts,), jnp.float32, smallest / len(cuts), high / len(cuts))
        return jnp.repeat(jnp.exp(steps), dims[dim] // parts).reshape((-1,) + (1,) * (len(dims) - dim - 1))

    level = one(*cuts[0])
    for cut in cuts[1:]:
        level = level * one(*cut)
    return level


def noise(own_key, extent, scale, reach, cuts=(), held_as=jnp.bfloat16):
    values = jax.random.normal(own_key, extent, jnp.float32) * scale
    if len(cuts) > 0:
        values = block_scale(own_key, extent, cuts, -0.22, 0.18) * values
    return jnp.clip(values, min=-reach, max=reach).astype(held_as)


def setup_inputs(seed: int = 0) -> dict:
    key_of = jax.random.split(jax.random.key(seed), 4)
    return {
        "intensity": noise(key_of[0], (BEAMS, CHAN, TIME), 1.0, 6.0, ((1, 512),), jnp.float32),
        "shift_table": draw_shift_table(jax.random.fold_in(key_of[3], 71), 0),
        "box_widths": draw_box_widths(jax.random.fold_in(key_of[3], 71), 0),
    }


def shift_rows(series, delays):
    length = series.shape[-1]
    moment = jnp.arange(length, dtype=jnp.int32)
    source = moment[None, :] + delays.astype(jnp.int32)[:, None]
    inside = source < length
    index = jnp.broadcast_to(jnp.minimum(source, length - 1), series.shape)
    picked = jnp.take_along_axis(series, index, axis=-1)
    return jnp.where(inside, picked, jnp.zeros_like(picked))

def merge_halves(lower, upper, delays):
    return jnp.repeat(lower, 2, axis=-2) + shift_rows(jnp.repeat(upper, 2, axis=-2), delays)

def box_peaks(plane, widths):
    length = plane.shape[-1]
    prefix = jnp.concatenate([jnp.zeros(plane.shape[:-1] + (1,), plane.dtype), jnp.cumsum(plane, axis=-1)], axis=-1)
    tail = jnp.broadcast_to(prefix[..., -1:], plane.shape[:-1] + (GTAPS,))
    padded = jnp.concatenate([prefix, tail], axis=-1)

    def single(width):
        ahead = lax.dynamic_slice_in_dim(padded, width, length, axis=padded.ndim - 1)
        return lax.optimization_barrier(jnp.max(ahead - prefix[..., :length], axis=-1)) / jnp.sqrt(width.astype(plane.dtype))
    return jax.vmap(single)(widths)

def gauss_taps(widths):
    taps = jnp.arange(GTAPS, dtype=jnp.float32)
    sigma = widths.astype(jnp.float32)[:, None] / 2.3548
    shape = jnp.exp(-0.5 * ((taps[None, :] - float(GTAPS // 2)) / sigma) ** 2)
    return shape / jnp.sqrt(lax.optimization_barrier(jnp.sum(shape * shape, axis=1, keepdims=True)))

def gauss_peaks(plane, taps):
    length = plane.shape[-1]
    span = 2 * length
    spectrum = jnp.fft.rfft(plane, n=span, axis=-1)
    kernel = jnp.fft.rfft(taps, n=span, axis=-1)
    filtered = jnp.fft.irfft(spectrum[None] * jnp.conj(kernel)[:, None], n=span, axis=-1)[..., :length]
    return lax.optimization_barrier(jnp.max(filtered, axis=-1)).astype(plane.dtype)

def reference(intensity, shift_table, box_widths):
    taps = gauss_taps(box_widths)
    nbits = N_SUB.bit_length() - 1
    listed = []
    for ident in range(N_SUB):
        value = 0
        for place in range(nbits):
            value = value | (ident >> place & 1) << nbits - 1 - place
        listed.append(value)
    order = jnp.array(listed, dtype=jnp.int32)
    scale = float(CHAN) ** (-0.5)

    def per_beam(channels):
        rows = lax.optimization_barrier(jnp.sum(channels.reshape(SUBS, GROUP, TIME), axis=1)) * scale
        size = 1
        for level in range(LEVELS):
            grouped = rows.reshape(SUBS // (2 * size), 2, size, TIME)
            rows = merge_halves(grouped[:, 0], grouped[:, 1], shift_table[level, :2 * size]).reshape(SUBS, TIME)
            size = size * 2
        plane = rows.reshape(N_SUB, SUBS // N_SUB, TIME)[order].reshape(SUBS, TIME)
        boxed = box_peaks(plane, box_widths)
        gaussed = gauss_peaks(plane, taps)
        return (plane, jnp.concatenate([boxed, gaussed], axis=0))
    planes, peaks = lax.map(per_beam, intensity)
    return (planes, peaks)
```

```python
import functools

import jax
import jax.numpy as jnp
from jax import lax
from jax.experimental import pallas as pl
from jax.experimental.pallas import tpu as pltpu
from jax.sharding import Mesh, PartitionSpec as P

GTAPS = 64
LANES = 128
F32 = jnp.float32
BF16 = jnp.bfloat16
SMEM = pltpu.SMEM
VMEM = pltpu.VMEM
LANEWISE = lax.GatherDimensionNumbers(
    offset_dims=(),
    collapsed_slice_dims=(1,),
    start_index_map=(1,),
    operand_batching_dims=(0,),
    start_indices_batching_dims=(0,),
)


def pick(block, index):
    return lax.gather(
        block, index[..., None], LANEWISE, (1, 1), mode=lax.GatherScatterMode.PROMISE_IN_BOUNDS
    )


def reversed_bits(value, bits):
    result = 0
    for place in range(bits):
        result = result + (value // (1 << place)) % 2 * (1 << (bits - 1 - place))
    return result


def iota(axis):
    return lax.broadcasted_iota(jnp.int32, (8, LANES), axis)


def delayed_pair(first, second, delay):
    source = iota(1) + delay
    index = source & (LANES - 1)
    near = source < LANES
    a = pick(first, index)
    b = pick(second, index)
    zero = jnp.zeros_like(a)
    return (
        jnp.where(near, a, jnp.where(source < 2 * LANES, b, zero)),
        jnp.where(near, b, zero),
    )


def merge_pair(lower, upper, delay):
    moved = delayed_pair(*upper, delay)
    return lower[0] + moved[0], lower[1] + moved[1]


def first_kernel(scale, table, x, out, split):
    beams = x.shape[0] // 16
    for half in range(2):
        split[half] = x[:, half * LANES : (half + 1) * LANES]
    for tile in range(beams // 8):
        subbands = []
        for s in range(4):
            halves = []
            for half in range(2):
                parts = [
                    split[half, pl.ds(tile * 128 + 4 * s + c, 8, stride=16), :]
                    for c in range(4)
                ]
                halves.append(((parts[0] + parts[1]) + (parts[2] + parts[3])) * scale)
            subbands.append(tuple(halves))
        pairs = [
            [merge_pair(subbands[2 * g], subbands[2 * g + 1], table[0, d]) for d in range(2)]
            for g in range(2)
        ]
        for target in range(4):
            d = (target & 1) * 2 + (target >> 1)
            row = merge_pair(pairs[0][d >> 1], pairs[1][d >> 1], table[1, d])
            for half in range(2):
                for j in range(4):
                    out[target * 8 + tile * 4 + j, 2 * half : 2 * half + 2, :] = row[half][
                        2 * j : 2 * j + 2, :
                    ]


class Delay:
    def __init__(self, low, high):
        lane, sublane = iota(1), iota(0)
        source = lane + jnp.where(sublane < 4, low, high)
        self.index = source & (LANES - 1)
        self.near = source < LANES
        self.next = (source < 2 * LANES) & ((sublane & 2) == 0)

    def __call__(self, block):
        a = pick(block, self.index)
        other = pltpu.roll(a, 6, 0)
        return jnp.where(self.near, a, jnp.where(self.next, other, jnp.zeros_like(a)))


def merge_blocks(blocks, bit, delay_of):
    delays = {}
    merged = [None] * len(blocks)
    for v in range(len(blocks)):
        kind = v & ((2 << bit) - 1)
        if kind not in delays:
            delays[kind] = delay_of(kind)
        merged[v] = blocks[v & ~(1 << bit)] + delays[kind](blocks[v | 1 << bit])
    return merged


def block_row(v, bits):
    return sum((v >> m & 1) << (bits - 1 - m) for m in range(bits))


def second_kernel(table, x, out):
    low = iota(0) < 4
    top = reversed_bits(lax.axis_index("x"), 2)
    delay = Delay(table[2, top * 2], table[2, top * 2 + 1])
    blocks = []
    for v in range(16):
        a = x[v]
        b = pltpu.roll(a, 4, 0)
        blocks.append(jnp.where(low, a, b) + delay(jnp.where(low, b, a)))
    for bit in range(4):
        base = top * (4 << bit)

        def delay_of(v, bit=bit, base=base):
            row = base + block_row(v, bit + 1)
            return Delay(table[bit + 3, row], table[bit + 3, row + (2 << bit)])

        blocks = merge_blocks(blocks, bit, delay_of)
    for w in range(8):
        a, b = blocks[w], blocks[8 + w]
        out[2 * w] = jnp.where(low, a, pltpu.roll(b, 4, 0))
        out[2 * w + 1] = jnp.where(low, pltpu.roll(a, 4, 0), b)


def prepare_kernel(table, widths, delays, box_gauss, gauss_rest):
    block = reversed_bits(lax.axis_index("x"), 2) * 16 + reversed_bits(lax.axis_index("z"), 4)
    for n in range(4):
        base = block * (4 << n)
        row = table[7 + n : 8 + n, pl.ds(pl.multiple_of(base // LANES * LANES, LANES), LANES)]
        delays[n : n + 1, :] = pltpu.roll(row, (LANES - base % LANES) % LANES, 1)
    shape = (GTAPS, LANES)
    lag = lax.broadcasted_iota(jnp.int32, shape, 1) - lax.broadcasted_iota(jnp.int32, shape, 0)
    valid = (lag >= 0) & (lag < GTAPS)
    offset = lag.astype(F32) - float(GTAPS // 2)
    for i in range(8):
        rows = pl.ds(i * GTAPS, GTAPS)
        ones = jnp.where((lag >= 0) & (lag < widths[i]), 1.0, 0.0).astype(BF16)
        box_gauss[rows, 0:LANES] = ones
        box_gauss[rows, LANES : 2 * LANES] = ones
        sigma = jnp.full(shape, widths[i], jnp.int32).astype(F32) / 2.3548
        taps = jnp.where(valid, jnp.exp(-0.5 * (offset / sigma) ** 2), 0.0)
        taps = taps / jnp.sqrt(jnp.sum(taps * taps, axis=1, keepdims=True))
        high = taps.astype(BF16)
        rows = pl.ds((8 + i) * GTAPS, GTAPS)
        box_gauss[rows, 0:LANES] = high
        box_gauss[rows, LANES : 2 * LANES] = high
        gauss_rest[pl.ds(i * GTAPS, GTAPS), :] = (taps - high.astype(F32)).astype(BF16)


def third_kernel(delays, widths, x, box_gauss, gauss_rest, plane, peaks, scratch):
    blocks = [x[v] for v in range(16)]
    for bit in range(4):

        def delay_of(v, bit=bit):
            row = block_row(v, bit + 1)
            return Delay(delays[bit, row], delays[bit, row + (2 << bit)])

        blocks = merge_blocks(blocks, bit, delay_of)
    for v in range(16):
        place = (v & 1) * 8 + block_row(v >> 1, 3)
        scratch[8 * place : 8 * place + 8, :] = blocks[v]
    halves = [[], []]
    for beam in range(2):
        for tile in range(4):
            for half in range(2):
                rows = scratch[
                    pl.ds((tile & 1) * 64 + (tile >> 1) * 4 + half * 2 + beam, 8, stride=8), :
                ]
                plane[beam, 8 * tile : 8 * tile + 8, half * LANES : (half + 1) * LANES] = rows
                halves[half].append(rows)
    first = jnp.concatenate(halves[0], axis=0)
    second = jnp.concatenate(halves[1], axis=0)
    early = lax.broadcasted_iota(jnp.int32, first.shape, 1) < GTAPS
    turned = pltpu.roll(second, GTAPS, 1)
    windows = jnp.concatenate(
        [
            first,
            jnp.where(early, pltpu.roll(first, GTAPS, 1), turned),
            second,
            jnp.where(early, turned, jnp.zeros_like(turned)),
        ],
        axis=0,
    )
    high = windows.astype(BF16)
    rest = (windows - high.astype(F32)).astype(BF16)
    both = jnp.concatenate([high, rest], axis=1)
    over = (((1,), (1,)), ((), ()))
    main = lax.dot_general(box_gauss[...], both, over, preferred_element_type=F32)
    small = lax.dot_general(gauss_rest[...], high, over, preferred_element_type=F32)
    best = []
    for i in range(16):
        value = main[i * GTAPS : (i + 1) * GTAPS]
        if i >= 8:
            value = value + small[(i - 8) * GTAPS : (i - 7) * GTAPS]
        value = jnp.maximum(value[:, :LANES], value[:, LANES:])
        value = jnp.max(value, axis=0, keepdims=True)
        if i < 8:
            value = value / jnp.sqrt(jnp.full(value.shape, widths[i], jnp.int32).astype(F32))
        best.append(value)
    best = jnp.concatenate(best, axis=0)
    best = jnp.maximum(best, pltpu.roll(best, GTAPS, 1))
    peaks[0] = best[:, :32]
    peaks[1] = pltpu.roll(best, LANES - 32, 1)[:, :32]


def whole(space=VMEM):
    return pl.BlockSpec(memory_space=space)


def shape_of(*dims, dtype=F32):
    return jax.ShapeDtypeStruct(dims, dtype)


def on_device(intensity, shift_table, box_widths):
    beams, channels, length = intensity.shape
    scale = float(channels * lax.axis_size(("z", "x", "beam"))) ** -0.5
    corner = pl.BlockSpec((8, LANES), lambda i: (0, 0), memory_space=SMEM)
    rows = pl.pallas_call(
        functools.partial(first_kernel, scale),
        grid=(1,),
        in_specs=[corner, pl.BlockSpec((beams * channels, length), lambda i: (0, 0))],
        out_specs=pl.BlockSpec((32, 4, LANES), lambda i: (0, 0, 0)),
        out_shape=shape_of(32, 4, LANES),
        scratch_shapes=[VMEM((2, beams * channels, LANES), F32)],
        name="channels_to_level_2",
    )(shift_table, intensity.reshape(beams * channels, length))
    rows = lax.all_to_all(rows, ("x", "beam"), split_axis=0, concat_axis=0, tiled=True)
    delays, box_gauss, gauss_rest = pl.pallas_call(
        prepare_kernel,
        in_specs=[whole(), whole(SMEM)],
        out_specs=[whole(), whole(), whole()],
        out_shape=[
            shape_of(4, LANES, dtype=jnp.int32),
            shape_of(16 * GTAPS, 2 * LANES, dtype=BF16),
            shape_of(8 * GTAPS, LANES, dtype=BF16),
        ],
        name="delays_and_taps",
    )(shift_table, box_widths)
    rows = pl.pallas_call(
        second_kernel,
        grid=(1,),
        in_specs=[corner, pl.BlockSpec((16, 8, LANES), lambda i: (0, 0, 0))],
        out_specs=pl.BlockSpec((16, 8, LANES), lambda i: (0, 0, 0)),
        out_shape=shape_of(16, 8, LANES),
        name="levels_3_to_7",
    )(shift_table, rows.reshape(16, 8, LANES))
    rows = lax.all_to_all(rows, "z", split_axis=0, concat_axis=0, tiled=True)
    return pl.pallas_call(
        third_kernel,
        in_specs=[whole(SMEM), whole(SMEM), whole(), whole(), whole()],
        out_specs=[whole(), whole()],
        out_shape=[shape_of(2, 32, length), shape_of(2, 16, 32)],
        scratch_shapes=[VMEM((LANES, LANES), F32)],
        name="levels_8_to_11_and_filters",
    )(delays, box_widths, rows, box_gauss, gauss_rest)


def solution(mesh):
    cube = Mesh(mesh.devices.reshape(16, 4, 8), ("z", "x", "beam"))
    in_specs = (P(None, ("z", "x", "beam"), None), P(), P())
    out_specs = (P("beam", ("z", "x"), None), P("beam", None, ("z", "x")))
    return jax.shard_map(
        on_device, mesh=cube, in_specs=in_specs, out_specs=out_specs, check_vma=False
    )
```

```python
import functools

import jax
import jax.numpy as jnp
from jax import lax
from jax.experimental import pallas as pl
from jax.experimental.pallas import tpu as pltpu
from jax.sharding import Mesh, PartitionSpec as P

GTAPS = 64
LANES = 128
F32 = jnp.float32
BF16 = jnp.bfloat16
PLANE_FIRST = 20
LINE_FIRST = 8
SMEM = pltpu.SMEM
VMEM = pltpu.VMEM
LANEWISE = lax.GatherDimensionNumbers(
    offset_dims=(),
    collapsed_slice_dims=(1,),
    start_index_map=(1,),
    operand_batching_dims=(0,),
    start_indices_batching_dims=(0,),
)


def pick(block, index):
    return lax.gather(
        block, index[..., None], LANEWISE, (1, 1), mode=lax.GatherScatterMode.PROMISE_IN_BOUNDS
    )


def reversed_bits(value, bits):
    result = 0
    for place in range(bits):
        result = result + (value // (1 << place)) % 2 * (1 << (bits - 1 - place))
    return result


def iota(axis):
    return lax.broadcasted_iota(jnp.int32, (8, LANES), axis)


def delayed_pair(first, second, delay):
    source = iota(1) + delay
    index = source & (LANES - 1)
    near = source < LANES
    a = pick(first, index)
    b = pick(second, index)
    zero = jnp.zeros_like(a)
    return (
        jnp.where(near, a, jnp.where(source < 2 * LANES, b, zero)),
        jnp.where(near, b, zero),
    )


def merge_pair(lower, upper, delay):
    moved = delayed_pair(*upper, delay)
    return lower[0] + moved[0], lower[1] + moved[1]


def first_kernel(scale, table, x, out, split):
    beams = x.shape[0] // 16
    for half in range(2):
        split[half] = x[:, half * LANES : (half + 1) * LANES]
    for tile in range(beams // 8):
        subbands = []
        for s in range(4):
            halves = []
            for half in range(2):
                parts = [
                    split[half, pl.ds(tile * 128 + 4 * s + c, 8, stride=16), :]
                    for c in range(4)
                ]
                halves.append(((parts[0] + parts[1]) + (parts[2] + parts[3])) * scale)
            subbands.append(tuple(halves))
        pairs = [
            [merge_pair(subbands[2 * g], subbands[2 * g + 1], table[0, d]) for d in range(2)]
            for g in range(2)
        ]
        for target in range(4):
            d = (target & 1) * 2 + (target >> 1)
            row = merge_pair(pairs[0][d >> 1], pairs[1][d >> 1], table[1, d])
            for half in range(2):
                for j in range(4):
                    out[(target * 8 + tile * 4 + j) ^ PLANE_FIRST, 2 * half : 2 * half + 2, :] = row[half][
                        2 * j : 2 * j + 2, :
                    ]


class Delay:
    def __init__(self, low, high):
        lane, sublane = iota(1), iota(0)
        source = lane + jnp.where(sublane < 4, low, high)
        self.index = source & (LANES - 1)
        self.near = source < LANES
        self.next = (source < 2 * LANES) & ((sublane & 2) == 0)

    def __call__(self, block):
        a = pick(block, self.index)
        other = pltpu.roll(a, 6, 0)
        return jnp.where(self.near, a, jnp.where(self.next, other, jnp.zeros_like(a)))


def merge_blocks(blocks, bit, delay_of):
    delays = {}
    merged = [None] * len(blocks)
    for v in range(len(blocks)):
        kind = v & ((2 << bit) - 1)
        if kind not in delays:
            delays[kind] = delay_of(kind)
        merged[v] = blocks[v & ~(1 << bit)] + delays[kind](blocks[v | 1 << bit])
    return merged


def block_row(v, bits):
    return sum((v >> m & 1) << (bits - 1 - m) for m in range(bits))


def second_kernel(table, x, out):
    low = iota(0) < 4
    top = reversed_bits(lax.axis_index("x"), 2)
    delay = Delay(table[2, top * 2], table[2, top * 2 + 1])
    blocks = []
    for v in range(16):
        a = x[v ^ PLANE_FIRST // 2]
        b = pltpu.roll(a, 4, 0)
        blocks.append(jnp.where(low, a, b) + delay(jnp.where(low, b, a)))
    for bit in range(4):
        base = top * (4 << bit)

        def delay_of(v, bit=bit, base=base):
            row = base + block_row(v, bit + 1)
            return Delay(table[bit + 3, row], table[bit + 3, row + (2 << bit)])

        blocks = merge_blocks(blocks, bit, delay_of)
    for w in range(8):
        a, b = blocks[w], blocks[8 + w]
        out[2 * w ^ LINE_FIRST] = jnp.where(low, a, pltpu.roll(b, 4, 0))
        out[2 * w + 1 ^ LINE_FIRST] = jnp.where(low, pltpu.roll(a, 4, 0), b)


def prepare_kernel(table, widths, delays, box_gauss, gauss_rest):
    block = reversed_bits(lax.axis_index("x"), 2) * 16 + reversed_bits(lax.axis_index("z"), 4)
    for n in range(4):
        base = block * (4 << n)
        row = table[7 + n : 8 + n, pl.ds(pl.multiple_of(base // LANES * LANES, LANES), LANES)]
        delays[n : n + 1, :] = pltpu.roll(row, (LANES - base % LANES) % LANES, 1)
    shape = (GTAPS, LANES)
    lag = lax.broadcasted_iota(jnp.int32, shape, 1) - lax.broadcasted_iota(jnp.int32, shape, 0)
    valid = (lag >= 0) & (lag < GTAPS)
    offset = lag.astype(F32) - float(GTAPS // 2)
    for i in range(8):
        rows = pl.ds(i * GTAPS, GTAPS)
        ones = jnp.where((lag >= 0) & (lag < widths[i]), 1.0, 0.0).astype(BF16)
        box_gauss[rows, 0:LANES] = ones
        box_gauss[rows, LANES : 2 * LANES] = ones
        sigma = jnp.full(shape, widths[i], jnp.int32).astype(F32) / 2.3548
        taps = jnp.where(valid, jnp.exp(-0.5 * (offset / sigma) ** 2), 0.0)
        taps = taps / jnp.sqrt(jnp.sum(taps * taps, axis=1, keepdims=True))
        high = taps.astype(BF16)
        rows = pl.ds((8 + i) * GTAPS, GTAPS)
        box_gauss[rows, 0:LANES] = high
        box_gauss[rows, LANES : 2 * LANES] = high
        gauss_rest[pl.ds(i * GTAPS, GTAPS), :] = (taps - high.astype(F32)).astype(BF16)


def third_kernel(delays, widths, x, box_gauss, gauss_rest, plane, peaks, scratch):
    blocks = [x[v ^ LINE_FIRST] for v in range(16)]
    for bit in range(4):

        def delay_of(v, bit=bit):
            row = block_row(v, bit + 1)
            return Delay(delays[bit, row], delays[bit, row + (2 << bit)])

        blocks = merge_blocks(blocks, bit, delay_of)
    for v in range(16):
        place = (v & 1) * 8 + block_row(v >> 1, 3)
        scratch[8 * place : 8 * place + 8, :] = blocks[v]
    halves = [[], []]
    for beam in range(2):
        for tile in range(4):
            for half in range(2):
                rows = scratch[
                    pl.ds((tile & 1) * 64 + (tile >> 1) * 4 + half * 2 + beam, 8, stride=8), :
                ]
                plane[beam, 8 * tile : 8 * tile + 8, half * LANES : (half + 1) * LANES] = rows
                halves[half].append(rows)
    first = jnp.concatenate(halves[0], axis=0)
    second = jnp.concatenate(halves[1], axis=0)
    early = lax.broadcasted_iota(jnp.int32, first.shape, 1) < GTAPS
    turned = pltpu.roll(second, GTAPS, 1)
    windows = jnp.concatenate(
        [
            first,
            jnp.where(early, pltpu.roll(first, GTAPS, 1), turned),
            second,
            jnp.where(early, turned, jnp.zeros_like(turned)),
        ],
        axis=0,
    )
    high = windows.astype(BF16)
    rest = (windows - high.astype(F32)).astype(BF16)
    both = jnp.concatenate([high, rest], axis=1)
    over = (((1,), (1,)), ((), ()))
    main = lax.dot_general(box_gauss[...], both, over, preferred_element_type=F32)
    small = lax.dot_general(gauss_rest[...], high, over, preferred_element_type=F32)
    best = []
    for i in range(16):
        value = main[i * GTAPS : (i + 1) * GTAPS]
        if i >= 8:
            value = value + small[(i - 8) * GTAPS : (i - 7) * GTAPS]
        value = jnp.maximum(value[:, :LANES], value[:, LANES:])
        value = jnp.max(value, axis=0, keepdims=True)
        if i < 8:
            value = value / jnp.sqrt(jnp.full(value.shape, widths[i], jnp.int32).astype(F32))
        best.append(value)
    best = jnp.concatenate(best, axis=0)
    best = jnp.maximum(best, pltpu.roll(best, GTAPS, 1))
    peaks[0] = best[:, :32]
    peaks[1] = pltpu.roll(best, LANES - 32, 1)[:, :32]


def exchanged(rows, axis, first):
    members = [place ^ first for place in range(lax.axis_size(axis))]
    return lax.all_to_all(
        rows, axis, split_axis=0, concat_axis=0, tiled=True, axis_index_groups=[members]
    )


def whole(space=VMEM):
    return pl.BlockSpec(memory_space=space)


def shape_of(*dims, dtype=F32):
    return jax.ShapeDtypeStruct(dims, dtype)


def on_device(intensity, shift_table, box_widths):
    beams, channels, length = intensity.shape
    scale = float(channels * lax.axis_size(("z", "x", "beam"))) ** -0.5
    corner = pl.BlockSpec((8, LANES), lambda i: (0, 0), memory_space=SMEM)
    rows = pl.pallas_call(
        functools.partial(first_kernel, scale),
        grid=(1,),
        in_specs=[corner, pl.BlockSpec((beams * channels, length), lambda i: (0, 0))],
        out_specs=pl.BlockSpec((32, 4, LANES), lambda i: (0, 0, 0)),
        out_shape=shape_of(32, 4, LANES),
        scratch_shapes=[VMEM((2, beams * channels, LANES), F32)],
        compiler_params=pltpu.CompilerParams(vmem_limit_bytes=8 << 20),
        name="channels_to_level_2",
    )(shift_table, intensity.reshape(beams * channels, length))
    rows = exchanged(rows, ("x", "beam"), PLANE_FIRST)
    delays, box_gauss, gauss_rest = pl.pallas_call(
        prepare_kernel,
        in_specs=[whole(), whole(SMEM)],
        out_specs=[whole(), whole(), whole()],
        out_shape=[
            shape_of(4, LANES, dtype=jnp.int32),
            shape_of(16 * GTAPS, 2 * LANES, dtype=BF16),
            shape_of(8 * GTAPS, LANES, dtype=BF16),
        ],
        compiler_params=pltpu.CompilerParams(vmem_limit_bytes=8 << 20),
        name="delays_and_taps",
    )(shift_table, box_widths)
    rows = pl.pallas_call(
        second_kernel,
        grid=(1,),
        in_specs=[corner, pl.BlockSpec((16, 8, LANES), lambda i: (0, 0, 0))],
        out_specs=pl.BlockSpec((16, 8, LANES), lambda i: (0, 0, 0)),
        out_shape=shape_of(16, 8, LANES),
        compiler_params=pltpu.CompilerParams(vmem_limit_bytes=8 << 20),
        name="levels_3_to_7",
    )(shift_table, rows.reshape(16, 8, LANES))
    rows = exchanged(rows, "z", LINE_FIRST)
    return pl.pallas_call(
        third_kernel,
        in_specs=[whole(SMEM), whole(SMEM), whole(), whole(), whole()],
        out_specs=[whole(), whole()],
        out_shape=[shape_of(2, 32, length), shape_of(2, 16, 32)],
        scratch_shapes=[VMEM((LANES, LANES), F32)],
        compiler_params=pltpu.CompilerParams(vmem_limit_bytes=8 << 20),
        name="levels_8_to_11_and_filters",
    )(delays, box_widths, rows, box_gauss, gauss_rest)


def solution(mesh):
    cube = Mesh(mesh.devices.reshape(16, 4, 8), ("z", "x", "beam"))
    in_specs = (P(None, ("z", "x", "beam"), None), P(), P())
    out_specs = (P("beam", ("z", "x"), None), P("beam", None, ("z", "x")))
    return jax.shard_map(
        on_device, mesh=cube, in_specs=in_specs, out_specs=out_specs, check_vma=False
    )
```

```python
import functools

import jax
import jax.numpy as jnp
from jax import lax
from jax.experimental import pallas as pl
from jax.experimental.pallas import tpu as pltpu
from jax.sharding import Mesh, PartitionSpec as P

GTAPS = 64
LANES = 128
F32 = jnp.float32
BF16 = jnp.bfloat16
PLANE_FIRST = 20
LINE_FIRST = 8
SMEM = pltpu.SMEM
VMEM = pltpu.VMEM
HBM = pltpu.HBM
LANEWISE = lax.GatherDimensionNumbers(
    offset_dims=(),
    collapsed_slice_dims=(1,),
    start_index_map=(1,),
    operand_batching_dims=(0,),
    start_indices_batching_dims=(0,),
)


def pick(block, index):
    return lax.gather(
        block, index[..., None], LANEWISE, (1, 1), mode=lax.GatherScatterMode.PROMISE_IN_BOUNDS
    )


def reversed_bits(value, bits):
    result = 0
    for place in range(bits):
        result = result + (value // (1 << place)) % 2 * (1 << (bits - 1 - place))
    return result


def iota(axis):
    return lax.broadcasted_iota(jnp.int32, (8, LANES), axis)


def delayed_pair(first, second, delay):
    source = iota(1) + delay
    index = source & (LANES - 1)
    near = source < LANES
    a = pick(first, index)
    b = pick(second, index)
    zero = jnp.zeros_like(a)
    return (
        jnp.where(near, a, jnp.where(source < 2 * LANES, b, zero)),
        jnp.where(near, b, zero),
    )


def merge_pair(lower, upper, delay):
    moved = delayed_pair(*upper, delay)
    return lower[0] + moved[0], lower[1] + moved[1]


def spread(row, place):
    return jnp.broadcast_to(row[:, place : place + 1], (8, LANES))


def first_kernel(scale, table, x, out, corner, split, corner_done, split_done):
    tiles = x.shape[0] // 128
    corner_copy = pltpu.make_async_copy(
        table.at[pl.ds(0, 8), pl.ds(0, LANES)], corner, corner_done
    )
    corner_copy.start()
    copies = []
    for tile in range(tiles):
        for half in range(2):
            copy = pltpu.make_async_copy(
                x.at[pl.ds(tile * 128, 128), pl.ds(half * LANES, LANES)],
                split.at[tile, half],
                split_done.at[tile, half],
            )
            copy.start()
            copies.append(copy)
    corner_copy.wait()
    first_delays = [spread(corner[0:1, :], d) for d in range(2)]
    second_delays = [spread(corner[1:2, :], d) for d in range(4)]
    for tile in range(tiles):
        copies[2 * tile].wait()
        copies[2 * tile + 1].wait()
        subbands = []
        for s in range(4):
            halves = []
            for half in range(2):
                parts = [split[tile, half, pl.ds(4 * s + c, 8, stride=16), :] for c in range(4)]
                halves.append(((parts[0] + parts[1]) + (parts[2] + parts[3])) * scale)
            subbands.append(tuple(halves))
        pairs = [
            [merge_pair(subbands[2 * g], subbands[2 * g + 1], first_delays[d]) for d in range(2)]
            for g in range(2)
        ]
        for target in range(4):
            d = (target & 1) * 2 + (target >> 1)
            row = merge_pair(pairs[0][d >> 1], pairs[1][d >> 1], second_delays[d])
            for half in range(2):
                for j in range(4):
                    place = (target * 8 + tile * 4 + j) ^ PLANE_FIRST
                    out[place, 2 * half : 2 * half + 2, :] = row[half][2 * j : 2 * j + 2, :]


def delayed(block, delay):
    source = iota(1) + delay
    a = pick(block, source & (LANES - 1))
    other = pltpu.roll(a, 6, 0)
    follows = (source < 2 * LANES) & ((iota(0) & 2) == 0)
    return jnp.where(source < LANES, a, jnp.where(follows, other, jnp.zeros_like(a)))


def merge_blocks(blocks, bit, delays, start):
    return [
        blocks[v & ~(1 << bit)]
        + delayed(blocks[v | 1 << bit], delays[start + (v & ((2 << bit) - 1))])
        for v in range(len(blocks))
    ]


def block_row(v, bits):
    return sum((v >> m & 1) << (bits - 1 - m) for m in range(bits))


def second_kernel(delays, x, out):
    low = iota(0) < 4
    blocks = []
    for v in range(16):
        a = x[v ^ PLANE_FIRST // 2]
        b = pltpu.roll(a, 4, 0)
        blocks.append(jnp.where(low, a, b) + delayed(jnp.where(low, b, a), delays[0]))
    for bit in range(4):
        blocks = merge_blocks(blocks, bit, delays, (2 << bit) - 1)
    for w in range(8):
        a, b = blocks[w], blocks[8 + w]
        out[2 * w ^ LINE_FIRST] = jnp.where(low, a, pltpu.roll(b, 4, 0))
        out[2 * w + 1 ^ LINE_FIRST] = jnp.where(low, pltpu.roll(a, 4, 0), b)


def prepare_kernel(table, widths, second, third, box_gauss, gauss_rest, box_scale):
    top = reversed_bits(lax.axis_index("x"), 2)
    block = top * 16 + reversed_bits(lax.axis_index("z"), 4)
    low = iota(0) < 4

    def level_row(level, base):
        row = table[level : level + 1, pl.ds(pl.multiple_of(base // LANES * LANES, LANES), LANES)]
        return pltpu.roll(row, (LANES - base % LANES) % LANES, 1)

    row = level_row(2, top * 2)
    second[0] = jnp.where(low, spread(row, 0), spread(row, 1))
    for bit in range(4):
        kinds = 2 << bit
        for out, row, start in (
            (second, level_row(3 + bit, top * 2 * kinds), kinds - 1),
            (third, level_row(7 + bit, block * 2 * kinds), kinds - 2),
        ):
            for v in range(kinds):
                d = block_row(v, bit + 1)
                out[start + v] = jnp.where(low, spread(row, d), spread(row, d + kinds))
    shape = (GTAPS, LANES)
    lag = lax.broadcasted_iota(jnp.int32, shape, 1) - lax.broadcasted_iota(jnp.int32, shape, 0)
    valid = (lag >= 0) & (lag < GTAPS)
    offset = lag.astype(F32) - float(GTAPS // 2)
    for i in range(8):
        rows = pl.ds(i * GTAPS, GTAPS)
        ones = jnp.where((lag >= 0) & (lag < widths[i]), 1.0, 0.0).astype(BF16)
        box_gauss[rows, 0:LANES] = ones
        box_gauss[rows, LANES : 2 * LANES] = ones
        width = jnp.full(shape, widths[i], jnp.int32).astype(F32)
        box_scale[i : i + 1, :] = jnp.sqrt(width[0:1, :])
        sigma = width / 2.3548
        taps = jnp.where(valid, jnp.exp(-0.5 * (offset / sigma) ** 2), 0.0)
        taps = taps / jnp.sqrt(jnp.sum(taps * taps, axis=1, keepdims=True))
        high = taps.astype(BF16)
        rows = pl.ds((8 + i) * GTAPS, GTAPS)
        box_gauss[rows, 0:LANES] = high
        box_gauss[rows, LANES : 2 * LANES] = high
        gauss_rest[pl.ds(i * GTAPS, GTAPS), :] = (taps - high.astype(F32)).astype(BF16)


def third_kernel(
    delays, box_scale, x, box_gauss, gauss_rest, plane, peaks, scratch, held, plane_done
):
    blocks = [x[v ^ LINE_FIRST] for v in range(16)]
    for bit in range(4):
        blocks = merge_blocks(blocks, bit, delays, (2 << bit) - 2)
    for v in range(16):
        place = (v & 1) * 8 + block_row(v >> 1, 3)
        scratch[8 * place : 8 * place + 8, :] = blocks[v]
    halves = [[], []]
    for beam in range(2):
        for tile in range(4):
            for half in range(2):
                rows = scratch[
                    pl.ds((tile & 1) * 64 + (tile >> 1) * 4 + half * 2 + beam, 8, stride=8), :
                ]
                held[beam, 8 * tile : 8 * tile + 8, half * LANES : (half + 1) * LANES] = rows
                halves[half].append(rows)
    copy = pltpu.make_async_copy(held, plane, plane_done)
    copy.start()
    first = jnp.concatenate(halves[0], axis=0)
    second = jnp.concatenate(halves[1], axis=0)
    early = lax.broadcasted_iota(jnp.int32, first.shape, 1) < GTAPS
    turned = pltpu.roll(second, GTAPS, 1)
    windows = jnp.concatenate(
        [
            first,
            jnp.where(early, pltpu.roll(first, GTAPS, 1), turned),
            second,
            jnp.where(early, turned, jnp.zeros_like(turned)),
        ],
        axis=0,
    )
    high = windows.astype(BF16)
    rest = (windows - high.astype(F32)).astype(BF16)
    both = jnp.concatenate([high, rest], axis=1)
    over = (((1,), (1,)), ((), ()))
    main = lax.dot_general(box_gauss[...], both, over, preferred_element_type=F32)
    small = lax.dot_general(gauss_rest[...], high, over, preferred_element_type=F32)
    best = []
    for i in range(16):
        value = main[i * GTAPS : (i + 1) * GTAPS]
        if i >= 8:
            value = value + small[(i - 8) * GTAPS : (i - 7) * GTAPS]
        value = jnp.maximum(value[:, :LANES], value[:, LANES:])
        value = jnp.max(value, axis=0, keepdims=True)
        best.append(value)
    best = jnp.concatenate(
        [jnp.concatenate(best[:8], axis=0) / box_scale[...], jnp.concatenate(best[8:], axis=0)],
        axis=0,
    )
    best = jnp.maximum(best, pltpu.roll(best, GTAPS, 1))
    peaks[0] = best[:, :32]
    peaks[1] = pltpu.roll(best, LANES - 32, 1)[:, :32]
    copy.wait()


def exchanged(rows, axis, first):
    members = [place ^ first for place in range(lax.axis_size(axis))]
    return lax.all_to_all(
        rows, axis, split_axis=0, concat_axis=0, tiled=True, axis_index_groups=[members]
    )


def whole(space=VMEM):
    return pl.BlockSpec(memory_space=space)


def shape_of(*dims, dtype=F32):
    return jax.ShapeDtypeStruct(dims, dtype)


def kernel_call(body, name, ins, outs, shapes, scratch=(), room=8):
    return pl.pallas_call(
        body,
        in_specs=[whole(space) for space in ins],
        out_specs=[whole(space) for space in outs],
        out_shape=shapes,
        scratch_shapes=list(scratch),
        compiler_params=pltpu.CompilerParams(vmem_limit_bytes=room << 20),
        name=name,
    )


def on_device(intensity, shift_table, box_widths):
    beams, channels, length = intensity.shape
    scale = float(channels * lax.axis_size(("z", "x", "beam"))) ** -0.5
    [rows] = kernel_call(
        functools.partial(first_kernel, scale),
        "channels_to_level_2",
        [HBM, HBM],
        [VMEM],
        [shape_of(32, 4, LANES)],
        [
            VMEM((8, LANES), jnp.int32),
            VMEM((beams // 8, 2, LANES, LANES), F32),
            pltpu.SemaphoreType.DMA,
            pltpu.SemaphoreType.DMA((beams // 8, 2)),
        ],
        room=60,
    )(shift_table, intensity.reshape(beams * channels, length))
    rows = exchanged(rows, ("x", "beam"), PLANE_FIRST)
    second, third, box_gauss, gauss_rest, box_scale = kernel_call(
        prepare_kernel,
        "delays_and_taps",
        [VMEM, SMEM],
        [VMEM] * 5,
        [
            shape_of(31, 8, LANES, dtype=jnp.int32),
            shape_of(30, 8, LANES, dtype=jnp.int32),
            shape_of(16 * GTAPS, 2 * LANES, dtype=BF16),
            shape_of(8 * GTAPS, LANES, dtype=BF16),
            shape_of(8, LANES),
        ],
    )(shift_table, box_widths)
    [rows] = kernel_call(
        second_kernel, "levels_3_to_7", [VMEM, VMEM], [VMEM], [shape_of(16, 8, LANES)]
    )(second, rows.reshape(16, 8, LANES))
    rows = exchanged(rows, "z", LINE_FIRST)
    return tuple(
        kernel_call(
            third_kernel,
            "levels_8_to_11_and_filters",
            [VMEM] * 5,
            [pl.ANY, VMEM],
            [shape_of(2, 32, length), shape_of(2, 16, 32)],
            [
                VMEM((LANES, LANES), F32),
                VMEM((2, 32, length), F32),
                pltpu.SemaphoreType.DMA,
            ],
        )(third, box_scale, rows, box_gauss, gauss_rest)
    )


def solution(mesh):
    cube = Mesh(mesh.devices.reshape(16, 4, 8), ("z", "x", "beam"))
    in_specs = (P(None, ("z", "x", "beam"), None), P(), P())
    out_specs = (P("beam", ("z", "x"), None), P("beam", None, ("z", "x")))
    return jax.shard_map(
        on_device, mesh=cube, in_specs=in_specs, out_specs=out_specs, check_vma=False
    )
```
